32 devices in a mesh: ctx: 8 (over z, x), tp: 4 (over y, core).
Axes of the slice: x: 2, y: 2, z: 4, core: 2. Of those that a mesh axis runs over, the one named last changes fastest.
Arguments:
- q_self: bfloat16 [1024, 4096], P('ctx', 'tp'), may hold values from -200 to 200
- k_self: bfloat16 [1024, 4096], P('ctx', 'tp'), may hold values from -7 to 7
- v_self: bfloat16 [1024, 4096], P('ctx', 'tp'), may hold values from -6 to 6
- window: int32 [32], replicated, may hold values from 16 to 64, as said below
- key_weight: bfloat16 [4096, 1024], P('tp'), may hold values from -0.28125 to 0.28125
- value_weight: bfloat16 [4096, 1024], P('tp'), may hold values from -0.28125 to 0.28125
- q_cross: bfloat16 [2, 1024, 4096], P(None, 'ctx', 'tp'), may hold values from -2000 to 2000
Outputs:
- self_mixed: bfloat16 [1024, 4096], P('ctx', 'tp')
- cross_mixed: bfloat16 [2, 1024, 4096], P(None, 'ctx', 'tp')
The draws below stay inside these ranges and needn't reach their ends.
Inputs may be any that keep to these rules, and one draw needn't show every extreme that they name: Every head's window lies between 16 and 64; some head has exactly 64.
All inputs are finite; a program needn't handle non-finite values.
Results may differ from the reference program's by a relative error of at most 0.025.
Values may be sent and summed in bfloat16 or wider, within the bound.
A program may use at most 64 MiB of HBM per device.

```python
import jax
import jax.numpy as jnp
from jax import lax

D = 4096
HEADS = 32
HEAD_DIM = 128
KV_HEADS = 8
LAYERS = 2
TOK_DEV = 128
STRETCH = 64
SEQ = 1024
N_CTX = 8


def paired_rows(key):
    base = jax.random.fold_in(key, 71)
    first, second = jax.random.split(base, 2)
    queries = jnp.clip(jax.random.normal(first, (SEQ, D), jnp.float32), -6.0, 6.0)
    keys = jnp.clip(jax.random.normal(second, (SEQ, D), jnp.float32), -6.0, 6.0)
    return (queries, keys)


def draw_q_self(key, part):
    return paired_rows(key)[0].astype(jnp.bfloat16)


def draw_k_self(key, part):
    return paired_rows(key)[1].astype(jnp.bfloat16)


def draw_window(key, part):
    spans = jax.random.randint(jax.random.fold_in(key, 5), (HEADS,), STRETCH // 4, STRETCH + 1)
    chosen = jax.random.randint(jax.random.fold_in(key, 6), (), 0, HEADS)
    return jnp.where(jnp.arange(HEADS) == chosen, STRETCH, spans).astype(jnp.int32)


def draw_q_cross(key, part):
    first = jax.random.fold_in(jax.random.fold_in(key, 13), 0)
    values = jnp.clip(jax.random.normal(first, (LAYERS, SEQ, D), jnp.float32), -6.0, 6.0)
    return values.astype(jnp.bfloat16)


def level_of(stream_key, shape, cuts, low, largest):
    gain = 1.0
    for axis_at, blocks in cuts:
        draws = jax.random.uniform(jax.random.fold_in(jax.random.fold_in(stream_key, 6), axis_at), (blocks,), jnp.float32, low / len(cuts), largest / len(cuts))
        gain = gain * jnp.repeat(jnp.exp(draws), shape[axis_at] // blocks).reshape((-1,) + (1,) * (len(shape) - 1 - axis_at))
    return gain


def normal_values(stream_key, shape, width, most, cuts=(), held_as=jnp.bfloat16):
    values = jax.random.normal(stream_key, shape, jnp.float32) * width
    if len(cuts) > 0:
        values = level_of(stream_key, shape, cuts, -0.22, 0.18) * values
    return jnp.clip(values, min=-most, max=most).astype(held_as)


def setup_inputs(seed: int = 0) -> dict:
    splits = jax.random.split(jax.random.key(seed), 8)
    return {
        "q_self": draw_q_self(jax.random.fold_in(splits[7], 71), 0),
        "k_self": draw_k_self(jax.random.fold_in(splits[7], 71), 0),
        "v_self": normal_values(splits[2], (SEQ, D), 1.0, 6.0, ((0, 8), (1, 4))),
        "window": draw_window(jax.random.fold_in(splits[7], 71), 0),
        "key_weight": normal_values(splits[4], (D, KV_HEADS * HEAD_DIM), (3.0 * D ** -0.5), 0.28125, ((0, 4),)),
        "value_weight": normal_values(splits[5], (D, KV_HEADS * HEAD_DIM), (3.0 * D ** -0.5), 0.28125, ((0, 4),)),
        "q_cross": draw_q_cross(jax.random.fold_in(splits[7], 71), 0),
    }


very_low = -1e30


def storage_positions():
    rows = jnp.arange(SEQ, dtype=jnp.int32)
    owner = rows // TOK_DEV
    within = rows % TOK_DEV
    stretch_id = jnp.where(within < STRETCH, owner, 2 * N_CTX - 1 - owner)
    return stretch_id * STRETCH + within % STRETCH


def natural_rows():
    places = jnp.arange(SEQ, dtype=jnp.int32)
    stretch_id = places // STRETCH
    owner = jnp.where(stretch_id < N_CTX, stretch_id, 2 * N_CTX - 1 - stretch_id)
    second = jnp.where(stretch_id < N_CTX, 0, 1)
    return (owner * TOK_DEV + second * STRETCH + places % STRETCH).astype(jnp.int32)


def weigh(scores, allowed, values, pattern):
    masked = jnp.where(allowed, scores, very_low)
    top = jnp.max(masked, axis=-1, keepdims=True)
    fresh = jnp.where(allowed, jnp.exp(masked - top), 0.0)
    total = jnp.sum(fresh, axis=-1, keepdims=True)
    rounded = fresh.astype(jnp.bfloat16).astype(jnp.float32)
    return jnp.einsum(pattern, rounded, values.astype(jnp.float32)), total


def reference(q_self, k_self, v_self, window, key_weight, value_weight, q_cross):
    scale = HEAD_DIM ** -0.5
    order = natural_rows()
    back = storage_positions()
    queries = q_self[order].reshape(SEQ, HEADS, HEAD_DIM)
    keys = k_self[order].reshape(SEQ, HEADS, HEAD_DIM)
    values = v_self[order].reshape(SEQ, HEADS, HEAD_DIM)
    filler = jnp.zeros((STRETCH, HEADS, HEAD_DIM), jnp.bfloat16)
    key_pad = jnp.concatenate([filler, keys], axis=0)
    value_pad = jnp.concatenate([filler, values], axis=0)

    def self_block(index):
        first = (index * STRETCH).astype(jnp.int32)
        query_rows = lax.dynamic_slice_in_dim(queries, first, STRETCH, 0)
        key_rows = lax.dynamic_slice_in_dim(key_pad, first, 2 * STRETCH, 0)
        value_rows = lax.dynamic_slice_in_dim(value_pad, first, 2 * STRETCH, 0)
        scores = jnp.einsum("qhd,khd->hqk", query_rows.astype(jnp.float32), key_rows.astype(jnp.float32)) * scale
        query_pos = first + jnp.arange(STRETCH, dtype=jnp.int32)
        key_pos = first - STRETCH + jnp.arange(2 * STRETCH, dtype=jnp.int32)
        gap = query_pos[:, None] - key_pos[None, :]
        allowed = (key_pos[None, :] >= 0) & (gap >= 0)
        allowed = allowed[None] & (gap[None] < window[:, None, None])
        summed, total = weigh(scores, allowed, value_rows, "hqk,khd->hqd")
        result = summed / total
        return jnp.transpose(result, (1, 0, 2)).reshape(STRETCH, D)

    blocks = lax.map(self_block, jnp.arange(SEQ // STRETCH, dtype=jnp.int32))
    self_natural = blocks.reshape(SEQ, D).astype(jnp.bfloat16)
    self_mixed = self_natural[back]
    cache_key = jnp.dot(self_mixed, key_weight, preferred_element_type=jnp.float32).astype(jnp.bfloat16)
    cache_value = jnp.dot(self_mixed, value_weight, preferred_element_type=jnp.float32).astype(jnp.bfloat16)
    group = HEADS // KV_HEADS
    key_nat = cache_key[order].reshape(SEQ, KV_HEADS, HEAD_DIM)
    value_nat = cache_value[order].reshape(SEQ, KV_HEADS, HEAD_DIM)
    key_pos = jnp.arange(SEQ, dtype=jnp.int32)
    outputs = []
    for layer in range(LAYERS):
        layer_q = q_cross[layer][order].reshape(SEQ, KV_HEADS, group, HEAD_DIM)

        def cross_block(index):
            first = (index * STRETCH).astype(jnp.int32)
            query_rows = lax.dynamic_slice_in_dim(layer_q, first, STRETCH, 0)
            scores = jnp.einsum("qagd,kad->agqk", query_rows.astype(jnp.float32), key_nat.astype(jnp.float32)) * scale
            query_pos = first + jnp.arange(STRETCH, dtype=jnp.int32)
            allowed = key_pos[None, :] <= query_pos[:, None]
            summed, total = weigh(scores, allowed, value_nat, "agqk,kad->agqd")
            result = summed / total
            return jnp.transpose(result, (2, 0, 1, 3)).reshape(STRETCH, D)

        cross_blocks = lax.map(cross_block, jnp.arange(SEQ // STRETCH, dtype=jnp.int32))
        outputs.append(cross_blocks.reshape(SEQ, D).astype(jnp.bfloat16)[back])
    return self_mixed, jnp.stack(outputs, axis=0)
```

```python
import functools
import math

import jax
import jax.numpy as jnp
from jax import lax
from jax.experimental import pallas as pl
from jax.experimental.pallas import tpu as pltpu
from jax.sharding import PartitionSpec as P

HEAD_DIM = 128
LOW = -1e30
MESH = pl.DeviceIdType.MESH
FACTOR = HEAD_DIM ** (-0.5) * math.log2(math.e)
NT = (((1,), (1,)), ((), ()))
TN = (((0,), (0,)), ((), ()))


def dot(a, b, dims=(((1,), (0,)), ((), ()))):
    return lax.dot_general(a, b, dims, preferred_element_type=jnp.float32)


def kernel(
    n, tpn, window, q_hbm, k_hbm, v_hbm, kw_hbm, vw_hbm, qc_hbm, self_hbm, cross_hbm,
    q, kcat, vcat, kw, vw, qc, mix, part_out, part_in, own, cache, qbuf,
    s1, s2, tops, sums, acc, out,
    load_sem, halo_send, halo_recv, rs_send, rs_recv, ag_send, ag_recv, out_sem,
):
    me = lax.axis_index("ctx")
    tp = lax.axis_index("tp")
    stretch = q.shape[0] // 2
    heads = q.shape[1] // HEAD_DIM
    layers = qc.shape[0]
    width = part_out.shape[-1] // 2
    kvh = width // HEAD_DIM
    group = heads // kvh
    rows = layers * group * stretch
    lines = n // 2
    z = me // 2
    xx = me % 2

    def load(number, src, dst):
        copy = pltpu.make_async_copy(src, dst, load_sem.at[number])
        copy.start()
        return copy

    both = [pl.ds(0, stretch), pl.ds(stretch, stretch)]
    loads = [load(0, q_hbm, q)]
    for b in range(2):
        loads.append(load(1 + b, k_hbm.at[both[b]], kcat.at[b, both[1]]))
        loads.append(load(3 + b, v_hbm.at[both[b]], vcat.at[b, both[1]]))
    load_w = [load(5, kw_hbm, kw), load(6, vw_hbm, vw)]
    load_c = load(7, qc_hbm, qc)

    barrier = pltpu.get_barrier_semaphore()
    for step in (-2, -1, 1, 2):
        ok = (me + step >= 0) & (me + step < n)

        @pl.when(ok)
        def _():
            pl.semaphore_signal(
                barrier, inc=1, device_id={"ctx": me + step, "tp": tp}, device_id_type=MESH
            )

    def flip(o):
        t = tp
        bit = 1
        while bit < tpn:
            if o & bit:
                t = t + bit - 2 * bit * ((tp // bit) % 2)
            bit *= 2
        return t

    for o in range(1, tpn):
        pl.semaphore_signal(
            barrier, inc=1, device_id={"ctx": me, "tp": flip(o)}, device_id_type=MESH
        )
    peers = tpn - 1
    for step in (1, 2):
        peers = peers + jnp.where(me >= step, 1, 0) + jnp.where(me + step < n, 1, 0)
    pl.semaphore_wait(barrier, peers)

    def halo(b, which):
        src, cat = ((k_hbm, kcat), (v_hbm, vcat))[which]
        return pltpu.make_async_remote_copy(
            src_ref=src.at[both[b]],
            dst_ref=cat.at[b, both[0]],
            send_sem=halo_send.at[b, which],
            recv_sem=halo_recv.at[b, which],
            device_id={"ctx": me + (1, -1)[b], "tp": tp},
            device_id_type=MESH,
        )

    sends_halo = (me < n - 1, me > 0)
    takes_halo = (me > 0, me < n - 1)
    for b in range(2):
        @pl.when(sends_halo[b])
        def _():
            halo(b, 0).start()
            halo(b, 1).start()

    for copy in loads:
        copy.wait()

    @pl.when(me == 0)
    def _():
        kcat[0, :stretch] = jnp.zeros((stretch, kcat.shape[2]), kcat.dtype)
        vcat[0, :stretch] = jnp.zeros((stretch, kcat.shape[2]), kcat.dtype)

    @pl.when(me == n - 1)
    def _():
        kcat[1, :stretch] = kcat[0, stretch:]
        vcat[1, :stretch] = vcat[0, stretch:]

    load_c.wait()
    for side in range(2):
        for a in range(kvh):
            for l in range(layers):
                for g in range(group):
                    at = (l * group + g) * stretch
                    h = a * group + g
                    qbuf[side, a, at : at + stretch] = qc[
                        l, side * stretch : (side + 1) * stretch, h * HEAD_DIM : (h + 1) * HEAD_DIM
                    ]

    gap = (
        lax.broadcasted_iota(jnp.int32, (stretch, 2 * stretch), 0)
        + stretch
        - lax.broadcasted_iota(jnp.int32, (stretch, 2 * stretch), 1)
    )

    def rs_copy(b, o):
        return pltpu.make_async_remote_copy(
            src_ref=part_out.at[b, o - 1],
            dst_ref=part_in.at[b, o - 1],
            send_sem=rs_send.at[b, o - 1],
            recv_sem=rs_recv.at[b, o - 1],
            device_id={"ctx": me, "tp": flip(o)},
            device_id_type=MESH,
        )

    for b in range(2):
        @pl.when(takes_halo[b])
        def _():
            halo(b, 0).wait_recv()
            halo(b, 1).wait_recv()

        if b == 0:
            most = jnp.where(me == 0, lax.broadcasted_iota(jnp.int32, gap.shape, 0), 2 * stretch)
        here = slice(b * stretch, (b + 1) * stretch)
        for h in range(heads):
            cols = slice(h * HEAD_DIM, (h + 1) * HEAD_DIM)
            s = dot(q[here, cols], kcat[b, :, cols], NT)
            allowed = (gap >= 0) & (gap < window[tp * heads + h])
            if b == 0:
                allowed = allowed & (gap <= most)
            s = jnp.where(allowed, s, LOW)
            top = jnp.max(s, axis=1, keepdims=True)
            p = jnp.exp2((s - top) * FACTOR)
            total = jnp.sum(p, axis=1, keepdims=True)
            o = dot(p.astype(jnp.bfloat16), vcat[b, :, cols])
            mix[here, cols] = (o / total).astype(jnp.bfloat16)
        if b == 0:
            for copy in load_w:
                copy.wait()
        x = mix[here, :]
        for o in [o for o in range(tpn - 1, 0, -1) if o != 1] + [1, 0]:
            if o >= tpn:
                continue
            cols = pl.ds(pl.multiple_of(flip(o) * width, HEAD_DIM), width)
            pk = dot(x, kw[:, cols])
            pv = dot(x, vw[:, cols])
            if o == 0:
                own[b, :, :width] = pk
                own[b, :, width:] = pv
            else:
                part_out[b, o - 1, :, :width] = pk.astype(jnp.bfloat16)
                part_out[b, o - 1, :, width:] = pv.astype(jnp.bfloat16)
                rs_copy(b, o).start()
    store_self = pltpu.make_async_copy(mix, self_hbm, out_sem.at[0])
    store_self.start()

    def ag_copy(part, owner, kind):
        target = (me + 2, me - 2, me + 1 - 2 * xx)[kind]
        return pltpu.make_async_remote_copy(
            src_ref=cache.at[part, owner],
            dst_ref=cache.at[part, owner],
            send_sem=ag_send.at[part, owner, kind],
            recv_sem=ag_recv.at[part, owner],
            device_id={"ctx": target, "tp": tp},
            device_id_type=MESH,
        )

    up, down = z < lines - 1, z > 0

    def plan(part, owner, where):
        if part == 0:
            if where == "own":
                return [(up, 0), (down, 1), (None, 2)]
            return [(up, 0), (None, 2)] if where == "below" else [(down, 1), (None, 2)]
        if where == "own":
            return [(down, 1), (xx == 1, 2)]
        return [(down, 1), (None, 2)]

    def act(part, owner, where, what):
        for cond, kind in plan(part, owner, where):
            if cond is None:
                getattr(ag_copy(part, owner, kind), what)()
            else:
                @pl.when(cond)
                def _():
                    getattr(ag_copy(part, owner, kind), what)()

    for b in range(2):
        value = own[b]
        for o in range(1, tpn):
            rs_copy(b, o).wait_recv()
            value = value + part_in[b, o - 1].astype(jnp.float32)
        cache[b, me] = value.astype(jnp.bfloat16)
        act(b, me, "own", "start")

    def forward(k, carry):
        @pl.when(z - k >= 0)
        def _():
            ag_copy(0, me - 2 * k, 2).wait_recv()
            act(0, me - 2 * k, "below", "start")

        @pl.when(z + k < lines)
        def _():
            for part in range(2):
                ag_copy(part, me + 2 * k, 2).wait_recv()
                act(part, me + 2 * k, "above", "start")

        return carry

    lax.fori_loop(1, lines, forward, 0)

    def collect(k, carry):
        owner = 2 * k + 1 - xx
        ag_copy(0, owner, 2).wait_recv()

        @pl.when((k > z) | ((k == z) & (xx == 0)))
        def _():
            ag_copy(1, owner, 2).wait_recv()

        return carry

    lax.fori_loop(0, lines, collect, 0)

    bunch = min(n, 8)
    deep = bunch * stretch
    slots = s1.shape[0]
    keep = (
        lax.broadcasted_iota(jnp.int32, (stretch, rows), 0)
        <= lax.broadcasted_iota(jnp.int32, (stretch, rows), 1) % stretch
    )

    def loop(count, body):
        if count <= 16:
            for i in range(count):
                body(i)
        else:
            lax.fori_loop(0, count, lambda i, c: (body(i), c)[1], 0)

    for first in range(0, kvh, slots):
        some = range(first, first + slots)
        for a in some:
            for side in range(2):
                tops[side, a] = jnp.full((1, rows), LOW, jnp.float32)
                sums[side, a] = jnp.zeros((1, rows), jnp.float32)
                acc[side, a] = jnp.zeros((HEAD_DIM, rows), jnp.float32)

        def wide_scores(i):
            for a in some:
                keys = cache[0, pl.ds(i * bunch, bunch), :, a * HEAD_DIM : (a + 1) * HEAD_DIM]
                s = dot(keys.reshape(deep, HEAD_DIM), qbuf[1, a], NT)
                s1[a - first, pl.ds(i * deep, deep)] = s
                tops[1, a] = jnp.maximum(tops[1, a], jnp.max(s, axis=0, keepdims=True))

        loop(n // bunch, wide_scores)

        def side_of(j):
            return jnp.where(j > me, 1, 0)

        def block_scores(j):
            side = side_of(j)
            free = (j != me) & (j != me + 1)
            for a in some:
                keys = cache[side, j - side, :, a * HEAD_DIM : (a + 1) * HEAD_DIM]
                s = dot(keys, qbuf[side, a], NT)
                s = jnp.where(keep | free, s, LOW)
                s2[a - first, pl.ds(j * stretch, stretch)] = s
                tops[side, a] = jnp.maximum(tops[side, a], jnp.max(s, axis=0, keepdims=True))

        loop(n + 1, block_scores)

        def wide_mix(i):
            for a in some:
                p = jnp.exp2((s1[a - first, pl.ds(i * deep, deep)] - tops[1, a]) * FACTOR)
                sums[1, a] += jnp.sum(p, axis=0, keepdims=True)
                values = cache[
                    0, pl.ds(i * bunch, bunch), :,
                    width + a * HEAD_DIM : width + (a + 1) * HEAD_DIM,
                ].reshape(deep, HEAD_DIM)
                acc[1, a] += dot(values, p.astype(jnp.bfloat16), TN)

        loop(n // bunch, wide_mix)

        def block_mix(j):
            side = side_of(j)
            for a in some:
                p = jnp.exp2((s2[a - first, pl.ds(j * stretch, stretch)] - tops[side, a]) * FACTOR)
                sums[side, a] += jnp.sum(p, axis=0, keepdims=True)
                values = cache[
                    side, j - side, :, width + a * HEAD_DIM : width + (a + 1) * HEAD_DIM
                ]
                acc[side, a] += dot(values, p.astype(jnp.bfloat16), TN)

        loop(n + 1, block_mix)

        for a in some:
            for side in range(2):
                o = (acc[side, a] / sums[side, a]).T.astype(jnp.bfloat16)
                for l in range(layers):
                    for g in range(group):
                        at = (l * group + g) * stretch
                        h = a * group + g
                        out[
                            l, side * stretch : (side + 1) * stretch,
                            h * HEAD_DIM : (h + 1) * HEAD_DIM,
                        ] = o[at : at + stretch]

    store_cross = pltpu.make_async_copy(out, cross_hbm, out_sem.at[1])
    store_cross.start()

    for b in range(2):
        @pl.when(sends_halo[b])
        def _():
            halo(b, 0).wait_send()
            halo(b, 1).wait_send()

        for o in range(1, tpn):
            rs_copy(b, o).wait_send()
        act(b, me, "own", "wait_send")

    def finish(k, carry):
        @pl.when(z - k >= 0)
        def _():
            act(0, me - 2 * k, "below", "wait_send")

        @pl.when(z + k < lines)
        def _():
            for part in range(2):
                act(part, me + 2 * k, "above", "wait_send")

        return carry

    lax.fori_loop(1, lines, finish, 0)
    store_self.wait()
    store_cross.wait()


def per_device(n, tpn, q_self, k_self, v_self, window, key_weight, value_weight, q_cross):
    tokens, columns = q_self.shape
    stretch = tokens // 2
    heads = columns // HEAD_DIM
    layers = q_cross.shape[0]
    width = key_weight.shape[1] // tpn
    kvh = width // HEAD_DIM
    rows = layers * (heads // kvh) * stretch
    slots = kvh if n <= 16 else 1
    bf, f32 = jnp.bfloat16, jnp.float32
    any_space = pl.BlockSpec(memory_space=pl.ANY)
    dma = pltpu.SemaphoreType.DMA
    return pl.pallas_call(
        functools.partial(kernel, n, tpn),
        out_shape=(
            jax.ShapeDtypeStruct(q_self.shape, bf),
            jax.ShapeDtypeStruct(q_cross.shape, bf),
        ),
        in_specs=[pl.BlockSpec(memory_space=pltpu.SMEM)] + [any_space] * 6,
        out_specs=(any_space, any_space),
        scratch_shapes=[
            pltpu.VMEM(q_self.shape, bf),
            pltpu.VMEM((2, tokens, columns), bf),
            pltpu.VMEM((2, tokens, columns), bf),
            pltpu.VMEM(key_weight.shape, bf),
            pltpu.VMEM(value_weight.shape, bf),
            pltpu.VMEM(q_cross.shape, bf),
            pltpu.VMEM(q_self.shape, bf),
            pltpu.VMEM((2, tpn - 1, stretch, 2 * width), bf),
            pltpu.VMEM((2, tpn - 1, stretch, 2 * width), bf),
            pltpu.VMEM((2, stretch, 2 * width), f32),
            pltpu.VMEM((2, n, stretch, 2 * width), bf),
            pltpu.VMEM((2, kvh, rows, HEAD_DIM), bf),
            pltpu.VMEM((slots, n * stretch, rows), f32),
            pltpu.VMEM((slots, (n + 1) * stretch, rows), f32),
            pltpu.VMEM((2, kvh, 1, rows), f32),
            pltpu.VMEM((2, kvh, 1, rows), f32),
            pltpu.VMEM((2, kvh, HEAD_DIM, rows), f32),
            pltpu.VMEM(q_cross.shape, bf),
            dma((8,)),
            dma((2, 2)),
            dma((2, 2)),
            dma((2, tpn - 1)),
            dma((2, tpn - 1)),
            dma((2, n, 3)),
            dma((2, n)),
            dma((2,)),
        ],
        compiler_params=pltpu.CompilerParams(
            collective_id=0, has_side_effects=True, vmem_limit_bytes=48 * 2**20
        ),
    )(window, q_self, k_self, v_self, key_weight, value_weight, q_cross)


def solution(mesh):
    n, tpn = mesh.shape["ctx"], mesh.shape["tp"]
    placed = (
        P("ctx", "tp"),
        P("ctx", "tp"),
        P("ctx", "tp"),
        P(),
        P("tp", None),
        P("tp", None),
        P(None, "ctx", "tp"),
    )
    return jax.shard_map(
        functools.partial(per_device, n, tpn),
        mesh=mesh,
        in_specs=placed,
        out_specs=(P("ctx", "tp"), P(None, "ctx", "tp")),
        check_vma=False,
    )
```

```python
import functools
import math

import jax
import jax.numpy as jnp
from jax import lax
from jax.experimental import pallas as pl
from jax.experimental.pallas import tpu as pltpu
from jax.sharding import PartitionSpec as P

HEAD_DIM = 128
LOW = -1e30
MESH = pl.DeviceIdType.MESH
FACTOR = HEAD_DIM ** (-0.5) * math.log2(math.e)
NT = (((1,), (1,)), ((), ()))
TN = (((0,), (0,)), ((), ()))


def dot(a, b, dims=(((1,), (0,)), ((), ()))):
    return lax.dot_general(a, b, dims, preferred_element_type=jnp.float32)


def kernel(
    n, tpn, window, q_hbm, k_hbm, v_hbm, kw_hbm, vw_hbm, qc_hbm, self_hbm, cross_hbm,
    q, kcat, vcat, kw, vw, qc, mix, part_out, part_in, own, cache, qbuf,
    tops, sums, acc, out,
    load_sem, halo_send, halo_recv, rs_send, rs_recv, line_send, cross_send, ag_recv, out_sem,
):
    me = lax.axis_index("ctx")
    tp = lax.axis_index("tp")
    stretch = q.shape[0] // 2
    heads = q.shape[1] // HEAD_DIM
    layers = qc.shape[0]
    width = part_out.shape[-1] // 2
    kvh = width // HEAD_DIM
    group = heads // kvh
    rows = layers * group * stretch
    lines = n // 2
    z = me // 2
    xx = me % 2

    def load(number, src, dst):
        copy = pltpu.make_async_copy(src, dst, load_sem.at[number])
        copy.start()
        return copy

    both = [pl.ds(0, stretch), pl.ds(stretch, stretch)]
    loads = [load(0, q_hbm, q)]
    for b in range(2):
        loads.append(load(1 + b, k_hbm.at[both[b]], kcat.at[b, both[1]]))
        loads.append(load(3 + b, v_hbm.at[both[b]], vcat.at[b, both[1]]))

    barrier = pltpu.get_barrier_semaphore()

    def greet(target):
        pl.semaphore_signal(
            barrier, inc=1, device_id={"ctx": target, "tp": tp}, device_id_type=MESH
        )

    for step in (-1, 1):
        @pl.when((me + step >= 0) & (me + step < n))
        def _():
            greet(me + step)

    def greet_line(k, carry):
        @pl.when(k != z)
        def _():
            greet(2 * k + xx)

        return carry

    lax.fori_loop(0, lines, greet_line, 0)

    def flip(o):
        t = tp
        bit = 1
        while bit < tpn:
            if o & bit:
                t = t + bit - 2 * bit * ((tp // bit) % 2)
            bit *= 2
        return t

    for o in range(1, tpn):
        pl.semaphore_signal(
            barrier, inc=1, device_id={"ctx": me, "tp": flip(o)}, device_id_type=MESH
        )
    peers = tpn - 1 + lines - 1 + jnp.where(me >= 1, 1, 0) + jnp.where(me + 1 < n, 1, 0)
    pl.semaphore_wait(barrier, peers)

    def halo(b, which):
        src, cat = ((k_hbm, kcat), (v_hbm, vcat))[which]
        return pltpu.make_async_remote_copy(
            src_ref=src.at[both[b]],
            dst_ref=cat.at[b, both[0]],
            send_sem=halo_send.at[b, which],
            recv_sem=halo_recv.at[b, which],
            device_id={"ctx": me + (1, -1)[b], "tp": tp},
            device_id_type=MESH,
        )

    sends_halo = (me < n - 1, me > 0)
    takes_halo = (me > 0, me < n - 1)
    def send_halo(b, what):
        @pl.when(sends_halo[b])
        def _():
            getattr(halo(b, 0), what)()
            getattr(halo(b, 1), what)()

    send_halo(0, "start")
    send_halo(1, "start")
    load_c = load(7, qc_hbm, qc)
    load_w = [load(5, kw_hbm, kw), load(6, vw_hbm, vw)]
    for copy in loads:
        copy.wait()

    @pl.when(me == 0)
    def _():
        kcat[0, :stretch] = jnp.zeros((stretch, kcat.shape[2]), kcat.dtype)
        vcat[0, :stretch] = jnp.zeros((stretch, kcat.shape[2]), kcat.dtype)

    @pl.when(me == n - 1)
    def _():
        kcat[1, :stretch] = kcat[0, stretch:]
        vcat[1, :stretch] = vcat[0, stretch:]

    load_c.wait()
    for side in range(2):
        for a in range(kvh):
            for l in range(layers):
                for g in range(group):
                    at = (l * group + g) * stretch
                    h = a * group + g
                    qbuf[side, a, at : at + stretch] = qc[
                        l, side * stretch : (side + 1) * stretch, h * HEAD_DIM : (h + 1) * HEAD_DIM
                    ]

    gap = (
        lax.broadcasted_iota(jnp.int32, (stretch, 2 * stretch), 0)
        + stretch
        - lax.broadcasted_iota(jnp.int32, (stretch, 2 * stretch), 1)
    )

    def rs_copy(b, o):
        return pltpu.make_async_remote_copy(
            src_ref=part_out.at[b, o - 1],
            dst_ref=part_in.at[b, o - 1],
            send_sem=rs_send.at[b, o - 1],
            recv_sem=rs_recv.at[b, o - 1],
            device_id={"ctx": me, "tp": flip(o)},
            device_id_type=MESH,
        )

    def clear(k, carry):
        cache[1, k] = jnp.zeros(cache.shape[2:], cache.dtype)
        return carry

    lax.fori_loop(0, me, clear, 0)

    def attend_self(b):
        @pl.when(takes_halo[b])
        def _():
            halo(b, 0).wait_recv()
            halo(b, 1).wait_recv()

        here = slice(b * stretch, (b + 1) * stretch)
        cols = [slice(h * HEAD_DIM, (h + 1) * HEAD_DIM) for h in range(heads)]
        base = (gap >= 0)
        if b == 0:
            own_row = lax.broadcasted_iota(jnp.int32, gap.shape, 0)
            base = base & (gap <= jnp.where(me == 0, own_row, 2 * stretch))
        s = [dot(q[here, c], kcat[b, :, c], NT) for c in cols]
        s = [
            jnp.where(base & (gap < window[tp * heads + h]), s[h], LOW) for h in range(heads)
        ]
        top = [jnp.max(t, axis=1, keepdims=True) for t in s]
        p = [jnp.exp2((t - m) * FACTOR) for t, m in zip(s, top)]
        total = [jnp.sum(t, axis=1, keepdims=True) for t in p]
        o = [dot(t.astype(jnp.bfloat16), vcat[b, :, c]) for t, c in zip(p, cols)]
        for c, t, m in zip(cols, o, total):
            mix[here, c] = (t / m).astype(jnp.bfloat16)

    def project(b):
        x = mix[b * stretch : (b + 1) * stretch, :]
        for o in [o for o in range(tpn - 1, 0, -1) if o != 1] + [1, 0]:
            if o >= tpn:
                continue
            cols = pl.ds(pl.multiple_of(flip(o) * width, HEAD_DIM), width)
            pk = dot(x, kw[:, cols])
            pv = dot(x, vw[:, cols])
            if o == 0:
                own[b, :, :width] = pk
                own[b, :, width:] = pv
            else:
                part_out[b, o - 1, :, :width] = pk.astype(jnp.bfloat16)
                part_out[b, o - 1, :, width:] = pv.astype(jnp.bfloat16)
                rs_copy(b, o).start()

    def ag_copy(part, owner, target, sem):
        return pltpu.make_async_remote_copy(
            src_ref=cache.at[part, owner],
            dst_ref=cache.at[part, owner],
            send_sem=sem,
            recv_sem=ag_recv.at[part, owner],
            device_id={"ctx": target, "tp": tp},
            device_id_type=MESH,
        )

    across = me + 1 - 2 * xx

    def line_copy(part, k):
        return ag_copy(part, me, 2 * k + xx, line_send.at[part, k])

    def cross_copy(part, k):
        return ag_copy(part, 2 * k + xx, across, cross_send.at[part, k])

    def own_cross(part, what):
        if part == 0:
            getattr(cross_copy(part, z), what)()
        else:
            @pl.when(xx == 1)
            def _():
                getattr(cross_copy(part, z), what)()

    def own_line(part, what):
        def body(i, carry):
            @pl.when(z - i >= 0)
            def _():
                getattr(line_copy(part, z - i), what)()

            if part == 0:
                @pl.when(z + i < lines)
                def _():
                    getattr(line_copy(part, z + i), what)()

            return carry

        lax.fori_loop(1, lines, body, 0)

    def gather_own(b):
        value = own[b]
        for o in range(1, tpn):
            rs_copy(b, o).wait_recv()
            value = value + part_in[b, o - 1].astype(jnp.float32)
        cache[b, me] = value.astype(jnp.bfloat16)
        own_cross(b, "start")
        own_line(b, "start")

    def forward(part, first, last):
        def body(i, carry):
            @pl.when(z + i < lines)
            def _():
                cross_copy(part, z + i).wait_recv()
                cross_copy(part, z + i).start()

            if part == 0:
                @pl.when(z - i >= 0)
                def _():
                    cross_copy(part, z - i).wait_recv()
                    cross_copy(part, z - i).start()

            return carry

        lax.fori_loop(first, last, body, 0)

    def collect(part):
        def body(k, carry):
            owner = 2 * k + 1 - xx

            def take():
                ag_copy(part, owner, across, cross_send.at[part, k]).wait_recv()

            if part == 0:
                take()
            else:
                pl.when((k > z) | ((k == z) & (xx == 0)))(take)
            return carry

        lax.fori_loop(0, lines, body, 0)

    bunch = min(n, 8)
    deep = bunch * stretch
    row = lax.broadcasted_iota(jnp.int32, (deep, rows), 0)
    keep_gap = (
        lax.broadcasted_iota(jnp.int32, (deep, rows), 1) % stretch - row % stretch
    )
    owner_of = row // stretch

    def fold(part, side, a, first):
        def body(i):
            at = pl.ds(i * bunch, bunch)
            keys = cache[part, at, :, a * HEAD_DIM : (a + 1) * HEAD_DIM]
            values = cache[part, at, :, width + a * HEAD_DIM : width + (a + 1) * HEAD_DIM]
            s = dot(keys.reshape(deep, HEAD_DIM), qbuf[side, a], NT)
            if part == side:
                ahead = me - i * bunch - owner_of
                if part == 1:
                    ahead = -ahead
                s = jnp.where((ahead > 0) | ((ahead == 0) & (keep_gap >= 0)), s, LOW)
            top = jnp.max(s, axis=0, keepdims=True)
            fresh = first and isinstance(i, int) and i == 0
            if not fresh:
                old = tops[side, a]
                top = jnp.maximum(old, top)
                factor = jnp.exp2((old - top) * FACTOR)
            p = jnp.exp2((s - top) * FACTOR)
            total = jnp.sum(p, axis=0, keepdims=True)
            added = dot(values.reshape(deep, HEAD_DIM), p.astype(jnp.bfloat16), TN)
            if not fresh:
                total = sums[side, a] * factor + total
                added = acc[side, a] * factor + added
            tops[side, a] = top
            sums[side, a] = total
            acc[side, a] = added

        count = n // bunch
        body(0)
        if count > 1:
            lax.fori_loop(1, count, lambda i, c: (body(i), c)[1], 0)

    def finish(side, a):
        o = (acc[side, a] / sums[side, a]).T.astype(jnp.bfloat16)
        for l in range(layers):
            for g in range(group):
                at = (l * group + g) * stretch
                h = a * group + g
                out[
                    l, side * stretch : (side + 1) * stretch, h * HEAD_DIM : (h + 1) * HEAD_DIM
                ] = o[at : at + stretch]

    attend_self(0)
    for copy in load_w:
        copy.wait()
    project(0)
    attend_self(1)
    store_self = pltpu.make_async_copy(mix, self_hbm, out_sem.at[0])
    store_self.start()
    gather_own(0)
    project(1)
    forward(0, 1, lines)
    gather_own(1)
    collect(0)
    for a in range(kvh):
        fold(0, 1, a, True)
    forward(1, 1, 2)
    for a in range(kvh):
        fold(0, 0, a, True)
        finish(0, a)
    forward(1, 2, lines)
    collect(1)
    for a in range(kvh):
        fold(1, 1, a, False)
    for a in range(kvh):
        finish(1, a)

    store_cross = pltpu.make_async_copy(out, cross_hbm, out_sem.at[1])
    store_cross.start()

    send_halo(0, "wait_send")
    send_halo(1, "wait_send")
    for b in range(2):
        for o in range(1, tpn):
            rs_copy(b, o).wait_send()
        own_cross(b, "wait_send")
        own_line(b, "wait_send")

        def sent(k, carry):
            @pl.when((k > z) if b == 1 else (k != z))
            def _():
                cross_copy(b, k).wait_send()

            return carry

        lax.fori_loop(0, lines, sent, 0)
    store_self.wait()
    store_cross.wait()


def per_device(n, tpn, q_self, k_self, v_self, window, key_weight, value_weight, q_cross):
    tokens, columns = q_self.shape
    stretch = tokens // 2
    heads = columns // HEAD_DIM
    layers = q_cross.shape[0]
    width = key_weight.shape[1] // tpn
    kvh = width // HEAD_DIM
    rows = layers * (heads // kvh) * stretch
    bf, f32 = jnp.bfloat16, jnp.float32
    any_space = pl.BlockSpec(memory_space=pl.ANY)
    dma = pltpu.SemaphoreType.DMA
    return pl.pallas_call(
        functools.partial(kernel, n, tpn),
        out_shape=(
            jax.ShapeDtypeStruct(q_self.shape, bf),
            jax.ShapeDtypeStruct(q_cross.shape, bf),
        ),
        in_specs=[pl.BlockSpec(memory_space=pltpu.SMEM)] + [any_space] * 6,
        out_specs=(any_space, any_space),
        scratch_shapes=[
            pltpu.VMEM(q_self.shape, bf),
            pltpu.VMEM((2, tokens, columns), bf),
            pltpu.VMEM((2, tokens, columns), bf),
            pltpu.VMEM(key_weight.shape, bf),
            pltpu.VMEM(value_weight.shape, bf),
            pltpu.VMEM(q_cross.shape, bf),
            pltpu.VMEM(q_self.shape, bf),
            pltpu.VMEM((2, tpn - 1, stretch, 2 * width), bf),
            pltpu.VMEM((2, tpn - 1, stretch, 2 * width), bf),
            pltpu.VMEM((2, stretch, 2 * width), f32),
            pltpu.VMEM((2, n, stretch, 2 * width), bf),
            pltpu.VMEM((2, kvh, rows, HEAD_DIM), bf),
            pltpu.VMEM((2, kvh, 1, rows), f32),
            pltpu.VMEM((2, kvh, 1, rows), f32),
            pltpu.VMEM((2, kvh, HEAD_DIM, rows), f32),
            pltpu.VMEM(q_cross.shape, bf),
            dma((8,)),
            dma((2, 2)),
            dma((2, 2)),
            dma((2, tpn - 1)),
            dma((2, tpn - 1)),
            dma((2, n // 2)),
            dma((2, n // 2)),
            dma((2, n)),
            dma((2,)),
        ],
        compiler_params=pltpu.CompilerParams(
            collective_id=0, has_side_effects=True, vmem_limit_bytes=60 * 2**20
        ),
    )(window, q_self, k_self, v_self, key_weight, value_weight, q_cross)


def solution(mesh):
    n, tpn = mesh.shape["ctx"], mesh.shape["tp"]
    placed = (
        P("ctx", "tp"),
        P("ctx", "tp"),
        P("ctx", "tp"),
        P(),
        P("tp", None),
        P("tp", None),
        P(None, "ctx", "tp"),
    )
    return jax.shard_map(
        functools.partial(per_device, n, tpn),
        mesh=mesh,
        in_specs=placed,
        out_specs=(P("ctx", "tp"), P(None, "ctx", "tp")),
        check_vma=False,
    )
```
